768 devices in a mesh: grid: 96 (over z, x, core), slab: 8 (over y).
Axes of the slice: x: 4, y: 8, z: 12, core: 2. Of those that a mesh axis runs over, the one named last changes fastest.
Arguments:
- user_index: int32 [6291456], P(('grid', 'slab')), may hold values from 0 to 511
- item_index: int32 [6291456], P(('grid', 'slab')), may hold values from 0 to 3071
- week_index: int32 [6291456], P(('grid', 'slab')), may hold values from 0 to 511
- counts: bfloat16 [6291456], P(('grid', 'slab')), may hold values from 1 to 16
- item_factor: bfloat16 [24576, 128], P(('grid', 'slab')), may hold values from 0 to 4.053116e-05
- week_factor: bfloat16 [512, 128], P('slab'), may hold values from 0 to 0.001953125
Outputs:
- user_factor: float32 [49152, 128], P(('grid', 'slab'))
The draws below stay inside these ranges and needn't reach their ends.
All inputs are finite; a program needn't handle non-finite values.
Results may differ from the reference program's by a relative error of at most 0.0043.
Values may be sent and summed in bfloat16 or wider, within the bound.
A program may use at most 32 MiB of HBM per device.

```python
import math
import jax
import jax.numpy as jnp
import numpy as np
from jax import lax

R = 128
K = 512
NNZ_DEV = 8192
U_DEV = 64
ITEM_DEV = 32
U_BLK = 512
I_BLK = 3072
ITEMS = 24576
NNZ = 6291456
N_GRID = 96
N_SLAB = 8


def touch_ends(entries, rng, smallest, high):
    dims = entries.shape
    place = [jax.random.randint(jax.random.fold_in(rng, axis), (), 0, dims[axis]) for axis in range(len(dims))]
    entries = entries.at[tuple(place)].set(smallest)
    longest = dims.index(max(dims))
    place[longest] = (place[longest] + 1) % dims[longest]
    return entries.at[tuple(place)].set(high)


def levels(stream_key, extent, shards, least, largest):
    gain = 1.0
    for position, shards_of in shards:
        draws = jax.random.uniform(jax.random.fold_in(jax.random.fold_in(stream_key, 6), position), (shards_of,), jnp.float32, least / len(shards), largest / len(shards))
        gain = gain * jnp.repeat(jnp.exp(draws), extent[position] // shards_of).reshape((-1,) + (1,) * (len(extent) - 1 - position))
    return gain


def rank_bounds(amount, skew):
    weights = [(1 << 20) // math.isqrt(standing ** skew) + 1 for standing in range(1, amount + 1)]
    scale = 1 + sum(weights) // (1 << 30)
    return np.cumsum(np.array([max(1, weight // scale) for weight in weights]))


def ranked(key, dims, count, slope):
    grid = rank_bounds(count, slope)
    lot = jax.random.randint(jax.random.fold_in(key, 1), dims, 0, int(grid[count - 1]))
    standing = jnp.searchsorted(jnp.asarray(grid, jnp.int32), lot, side="right")
    return jax.random.permutation(jax.random.fold_in(key, 2), count)[standing].astype(jnp.int32)


def setup_inputs(seed: int = 0) -> dict:
    key_list = jax.random.split(jax.random.key(seed), 7)
    user_index = touch_ends(ranked(key_list[0], (NNZ,), U_BLK, 2), jax.random.fold_in(key_list[0], 3), 0, U_BLK - 1).astype(jnp.int32)
    item_index = touch_ends(jax.random.randint(key_list[1], (NNZ,), 0, I_BLK), jax.random.fold_in(key_list[1], 1), 0, I_BLK - 1).astype(jnp.int32)
    week_index = touch_ends(jax.random.randint(key_list[2], (NNZ,), 0, K), jax.random.fold_in(key_list[2], 1), 0, K - 1).astype(jnp.int32)
    counts = jnp.clip(jnp.exp(math.log(16.0) - 2.7725887 * jax.random.uniform(key_list[3], (NNZ,), jnp.float32) ** levels(key_list[3], (NNZ,), ((0, 768),), -0.2, 0.2)), 1.0, 16.0).astype(jnp.bfloat16)
    item_factor = jnp.clip(4.0531158447265625e-05 * jax.random.uniform(key_list[4], (ITEMS, R), jnp.float32) ** levels(key_list[4], (ITEMS, R), ((0, 768),), -0.2, 0.2), 0.0, 4.0531158447265625e-05).astype(jnp.bfloat16)
    week_factor = jnp.clip(0.001953125 * jax.random.uniform(key_list[5], (K, R), jnp.float32) ** levels(key_list[5], (K, R), ((0, 8),), -0.2, 0.2), 0.0, 0.001953125).astype(jnp.bfloat16)
    return dict(user_index=user_index, item_index=item_index, week_index=week_index, counts=counts, item_factor=item_factor, week_factor=week_factor)


def solve_rows(gram, rows):
    factor = jnp.linalg.cholesky(gram)
    middle = lax.linalg.triangular_solve(factor, rows, left_side=False, lower=True, transpose_a=True)
    return lax.linalg.triangular_solve(factor, middle, left_side=False, lower=True, transpose_a=False)

def reference(user_index, item_index, week_index, counts, item_factor, week_factor):
    devices = N_GRID * N_SLAB
    u_blk = U_DEV * N_SLAB

    def per_device(total, device):
        start = device * NNZ_DEV
        users = lax.dynamic_slice_in_dim(user_index, start, NNZ_DEV)
        items = lax.dynamic_slice_in_dim(item_index, start, NNZ_DEV)
        weeks = lax.dynamic_slice_in_dim(week_index, start, NNZ_DEV)
        values = lax.dynamic_slice_in_dim(counts, start, NNZ_DEV)
        group = (device // N_SLAB).astype(jnp.int32)
        slabpos = (device % N_SLAB).astype(jnp.int32)
        rows = (items // ITEM_DEV * N_SLAB + slabpos) * ITEM_DEV + items % ITEM_DEV
        picked = item_factor[rows].astype(jnp.float32)
        weekly = week_factor[weeks].astype(jnp.float32)
        kr_rows = (values.astype(jnp.float32)[:, None] * picked * weekly).astype(jnp.bfloat16)
        part = jax.ops.segment_sum(kr_rows.astype(jnp.float32), users, num_segments=u_blk)
        offset = (group * u_blk).astype(jnp.int32)
        block = lax.dynamic_slice_in_dim(total, offset, u_blk, 0)
        total = lax.dynamic_update_slice_in_dim(total, block + part, offset, 0)
        return (total, None)
    start_total = jnp.zeros((U_DEV * devices, R), jnp.float32)
    mttkrp, _ = lax.scan(per_device, start_total, jnp.arange(devices, dtype=jnp.int32))
    item_gram = jnp.dot(item_factor.T.astype(jnp.float32), item_factor.astype(jnp.float32), preferred_element_type=jnp.float32)
    week_gram = jnp.dot(week_factor.T.astype(jnp.float32), week_factor.astype(jnp.float32), preferred_element_type=jnp.float32)
    gram = item_gram * week_gram
    return solve_rows(gram, mttkrp)
```

```python
import functools

import jax
import jax.numpy as jnp
from jax import lax
from jax.experimental import pallas as pl
from jax.experimental.pallas import tpu as pltpu
from jax.sharding import PartitionSpec as P

MESH = pl.DeviceIdType.MESH
N_X = 4
N_CORE = 2
HI = 4
WEEK_HI = 2
LANES = 128
N_BLK = 1024
PANEL = 32
F32 = jnp.float32
BF16 = jnp.bfloat16


def select_ones(row, table):
    h = table.shape[0]
    packed = jnp.broadcast_to(row, (16, LANES)).astype(jnp.int16)
    packed = jnp.concatenate([packed] * (h // 16), 0)
    return jnp.where(packed == table, BF16(1), BF16(0))


def dot_nt(a, b, **kw):
    return lax.dot_general(a, b, (((1,), (1,)), ((), ())), preferred_element_type=F32, **kw)


def dot_tn(a, b, **kw):
    return lax.dot_general(a, b, (((0,), (0,)), ((), ())), preferred_element_type=F32, **kw)


def invert_spd(a):
    n = a.shape[0]
    lane = lax.broadcasted_iota(jnp.int32, (PANEL, n), 1)
    sub = lax.broadcasted_iota(jnp.int32, (PANEL, n), 0)
    wide_lane = lax.broadcasted_iota(jnp.int32, (n, n), 1)

    def sweep(_, a):
        panel = a[:PANEL]
        x = panel
        for j in range(PANEL):
            at = lane == j
            col = jnp.broadcast_to(x[:, j : j + 1], (PANEL, n))
            inv = 1.0 / col[j : j + 1]
            row = jnp.where(at[:1], inv, x[j : j + 1] * inv)
            x = jnp.where(
                sub == j,
                jnp.broadcast_to(row, (PANEL, n)),
                jnp.where(at, 0.0, x) - col * row,
            )
        r = jnp.where(lane < PANEL, -x, x)
        rest = jnp.where(wide_lane < PANEL, 0.0, a) - dot_tn(panel, r, precision=lax.Precision.HIGHEST)
        a = jnp.concatenate([rest[PANEL:], r], 0)
        return pltpu.roll(a, n - PANEL, 1)

    return -lax.fori_loop(0, n // PANEL, sweep, a)


def kernel(
    n_z, n_y,
    user_ref, item_ix_ref, week_ix_ref, count_ref, item_ref, week_ref, out_ref,
    table, weeks, hot_item, hot_user, scaled, tt, wt, iota, hi, lo,
    total, gram_part, gram_in, gram_sum, gram_all, rows_in,
    z_send, z_recv, x_send, x_recv, c_send, c_recv, w_send, w_recv,
    g_send, g_recv, h_send, h_recv, m_send, m_recv,
):
    g = lax.axis_index("grid")
    s = lax.axis_index("slab")
    z = g // (N_X * N_CORE)
    x = (g // N_CORE) % N_X
    c = g % N_CORE
    rank = item_ref.shape[1]
    per = item_ref.shape[0]
    groups = user_ref.shape[0]
    n_all = groups * LANES
    users = hot_user.shape[0]
    n_lo = hot_item.shape[0]
    n_week = weeks.shape[0] * weeks.shape[1]

    def grid_id(zz, xx, cc):
        return (zz * N_X + xx) * N_CORE + cc

    def z_at(d):
        return lax.rem(z + d, n_z)

    def x_at(d):
        return lax.rem(x + d, N_X)

    def y_at(d):
        return lax.rem(s + d, n_y)

    z_peers = [(grid_id(z_at(d), x, c), s) for d in range(1, n_z)]
    x_peers = [(grid_id(z, x_at(d), c), s) for d in range(1, N_X)]
    c_peer = (grid_id(z, x, 1 - c), s)
    y_peers = [(g, y_at(d)) for d in range(1, n_y)]

    barrier = pltpu.get_barrier_semaphore()
    partners = z_peers + x_peers + [c_peer] + y_peers
    for who in partners:
        pl.semaphore_signal(barrier, inc=1, device_id=who, device_id_type=MESH)

    l = item_ix_ref[...]
    grid_of = lax.shift_right_logical(l, per.bit_length() - 1)
    l_z = lax.shift_right_logical(grid_of, 3)
    l_x = lax.shift_right_logical(grid_of, 1) & 3
    hi[...] = (grid_of & 1) * 2 + lax.shift_right_logical(l_x, 1)
    lo[...] = ((l_x & 1) * n_z + l_z) * per + (l & (per - 1))
    iota[...] = lax.broadcasted_iota(jnp.int32, iota.shape, 0).astype(jnp.int16)

    pl.semaphore_wait(barrier, len(partners))

    pending = []

    def send(src, dst, send_sem, recv_sem, who):
        copy = pltpu.make_async_remote_copy(
            src_ref=src, dst_ref=dst, send_sem=send_sem, recv_sem=recv_sem,
            device_id=who, device_id_type=MESH,
        )
        copy.start()
        pending.append(copy)

    def arrived(dst, send_sem, recv_sem, who):
        pltpu.make_async_remote_copy(
            src_ref=dst, dst_ref=dst, send_sem=send_sem, recv_sem=recv_sem,
            device_id=who, device_id_type=MESH,
        ).wait_recv()

    for d in range(1, n_z):
        send(item_ref, table.at[c, x, z], z_send.at[d - 1], z_recv.at[d - 1], z_peers[d - 1])
    for d in range(1, n_y):
        send(week_ref, weeks.at[s], w_send.at[d - 1], w_recv.at[d - 1], y_peers[d - 1])
    table[c, x, z] = item_ref[...]
    weeks[s] = week_ref[...]

    def make_user(r, carry):
        col = pl.ds(pl.multiple_of(r * LANES, LANES), LANES)
        hot_user[:, col] = select_ones(user_ref[pl.ds(r, 1), :], iota[:users])
        return carry

    lax.fori_loop(0, groups, make_user, 0)

    for d in range(1, n_z):
        arrived(table.at[c, x, z_at(n_z - d)], z_send.at[d - 1], z_recv.at[d - 1], z_peers[d - 1])
    for d in range(1, N_X):
        send(table.at[c, x], table.at[c, x], x_send.at[d - 1], x_recv.at[d - 1], x_peers[d - 1])
    send(table.at[c, x], table.at[c, x], c_send.at[0], c_recv.at[0], c_peer)

    def make_item(r, carry):
        col = pl.ds(pl.multiple_of(r * LANES, LANES), LANES)
        hot_item[:, col] = select_ones(lo[pl.ds(r, 1), :], iota[:n_lo])
        return carry

    lax.fori_loop(0, groups, make_item, 0)

    for d in range(1, N_X):
        spot = table.at[c, x_at(N_X - d)]
        arrived(spot, x_send.at[d - 1], x_recv.at[d - 1], x_peers[d - 1])
        send(spot, spot, c_send.at[d], c_recv.at[d], c_peer)

    eye = jnp.where(
        lax.broadcasted_iota(jnp.int32, (rank, rank), 0)
        == lax.broadcasted_iota(jnp.int32, (rank, rank), 1),
        1.0, 0.0,
    ).astype(BF16)

    for d in range(1, n_y):
        arrived(weeks.at[y_at(n_y - d)], w_send.at[d - 1], w_recv.at[d - 1], y_peers[d - 1])
    n_wlo = n_week // WEEK_HI
    for j in range(WEEK_HI):
        each = weeks.shape[0] // WEEK_HI
        part = weeks[j * each : (j + 1) * each].reshape(n_wlo, rank)
        wt[j * rank : (j + 1) * rank, :] = dot_nt(eye, part).astype(BF16)
    week_gram = dot_nt(wt[:rank], wt[:rank])
    for j in range(1, WEEK_HI):
        week_gram += dot_nt(wt[j * rank : (j + 1) * rank], wt[j * rank : (j + 1) * rank])

    per_blk = N_BLK // LANES

    def week_block(k, carry):
        hots = []
        for q in range(per_blk):
            w = week_ix_ref[pl.ds(k * per_blk + q, 1), :]
            hots.append(select_ones(w & (n_wlo - 1), iota[:n_wlo]))
        looked = jnp.dot(wt[...], jnp.concatenate(hots, 1), preferred_element_type=F32)
        for q in range(per_blk):
            w = week_ix_ref[pl.ds(k * per_blk + q, 1), :]
            top = jnp.broadcast_to(lax.shift_right_logical(w, n_wlo.bit_length() - 1), (rank, LANES))
            part = looked[:, q * LANES : (q + 1) * LANES]
            value = part[(WEEK_HI - 1) * rank :]
            for j in range(WEEK_HI - 2, -1, -1):
                value = jnp.where(top == j, part[j * rank : (j + 1) * rank], value)
            count = count_ref[pl.ds(k * per_blk + q, 1), :]
            col = pl.ds(pl.multiple_of(k * N_BLK + q * LANES, LANES), LANES)
            scaled[:, col] = value * count
        return carry

    lax.fori_loop(0, n_all // N_BLK, week_block, 0)

    for d in range(N_X):
        spot = table.at[1 - c, x_at((N_X - d) % N_X)]
        arrived(spot, c_send.at[d], c_recv.at[d], c_peer)

    half = N_X * N_CORE // HI
    item_gram = None
    for j in range(HI):
        first = (j * half) % N_X
        part = table[(j * half) // N_X, first : first + half].reshape(n_lo, rank)
        columns = dot_nt(eye, part).astype(BF16)
        tt[j * rank : (j + 1) * rank, :] = columns
        term = dot_nt(columns, columns)
        item_gram = term if item_gram is None else item_gram + term
    gram_part[...] = item_gram.reshape(gram_part.shape)
    for d in range(1, n_y):
        send(gram_part.at[y_at(d)], gram_in.at[d - 1], g_send.at[d - 1], g_recv.at[d - 1], y_peers[d - 1])

    total[...] = jnp.zeros_like(total)

    def main_block(k, carry):
        col = pl.ds(pl.multiple_of(k * N_BLK, N_BLK), N_BLK)
        looked = jnp.dot(tt[...], hot_item[:, col], preferred_element_type=F32)
        kr = []
        for q in range(per_blk):
            top = jnp.broadcast_to(hi[pl.ds(k * per_blk + q, 1), :], (rank, LANES))
            part = looked[:, q * LANES : (q + 1) * LANES]
            value = part[(HI - 1) * rank :]
            for j in range(HI - 2, -1, -1):
                value = jnp.where(top == j, part[j * rank : (j + 1) * rank], value)
            at = pl.ds(pl.multiple_of(k * N_BLK + q * LANES, LANES), LANES)
            kr.append((value * scaled[:, at]).astype(BF16))
        add = dot_nt(hot_user[:, col], jnp.concatenate(kr, 1))
        total[...] += add.reshape(total.shape)
        return carry

    blocks = n_all // N_BLK
    lax.fori_loop(0, blocks // 2, main_block, 0)

    for d in range(1, n_y):
        arrived(gram_in.at[d - 1], g_send.at[d - 1], g_recv.at[d - 1], y_peers[d - 1])
    piece = gram_part[s]
    for d in range(1, n_y):
        piece = piece + gram_in[d - 1]
    gram_sum[...] = piece
    gram_all[s] = piece
    for d in range(1, n_y):
        send(gram_sum, gram_all.at[s], h_send.at[d - 1], h_recv.at[d - 1], y_peers[d - 1])

    lax.fori_loop(blocks // 2, blocks, main_block, 0)

    for d in range(1, n_y):
        send(total.at[y_at(d)], rows_in.at[d - 1], m_send.at[d - 1], m_recv.at[d - 1], y_peers[d - 1])

    for d in range(1, n_y):
        arrived(gram_all.at[y_at(n_y - d)], h_send.at[d - 1], h_recv.at[d - 1], y_peers[d - 1])
    inverse = invert_spd(gram_all[...].reshape(rank, rank) * week_gram)

    for d in range(1, n_y):
        arrived(rows_in.at[d - 1], m_send.at[d - 1], m_recv.at[d - 1], y_peers[d - 1])
    rows = total[s]
    for d in range(1, n_y):
        rows = rows + rows_in[d - 1]
    out_ref[...] = jnp.dot(rows, inverse, preferred_element_type=F32, precision=lax.Precision.HIGHEST)

    for copy in pending:
        copy.wait_send()


def local(n_grid, n_y, user_index, item_index, week_index, counts, item_factor, week_factor):
    n_all = user_index.shape[0]
    groups = n_all // LANES
    per, rank = item_factor.shape
    n_z = n_grid // (N_X * N_CORE)
    n_item = per * n_grid
    n_lo = n_item // HI
    n_week = week_factor.shape[0] * n_y
    u_dev = 64
    users = u_dev * n_y
    dma = pltpu.SemaphoreType.DMA
    return pl.pallas_call(
        functools.partial(kernel, n_z, n_y),
        out_shape=jax.ShapeDtypeStruct((u_dev, rank), F32),
        in_specs=[pl.BlockSpec(memory_space=pltpu.VMEM)] * 6,
        out_specs=pl.BlockSpec(memory_space=pltpu.VMEM),
        scratch_shapes=[
            pltpu.VMEM((N_CORE, N_X, n_z, per, rank), BF16),
            pltpu.VMEM((n_y,) + week_factor.shape, BF16),
            pltpu.VMEM((n_lo, n_all), BF16),
            pltpu.VMEM((users, n_all), BF16),
            pltpu.VMEM((rank, n_all), F32),
            pltpu.VMEM((HI * rank, n_lo), BF16),
            pltpu.VMEM((WEEK_HI * rank, n_week // WEEK_HI), BF16),
            pltpu.VMEM((max(n_lo, users), LANES), jnp.int16),
            pltpu.VMEM((groups, LANES), jnp.int32),
            pltpu.VMEM((groups, LANES), jnp.int32),
            pltpu.VMEM((n_y, u_dev, rank), F32),
            pltpu.VMEM((n_y, rank // n_y, rank), F32),
            pltpu.VMEM((n_y - 1, rank // n_y, rank), F32),
            pltpu.VMEM((rank // n_y, rank), F32),
            pltpu.VMEM((n_y, rank // n_y, rank), F32),
            pltpu.VMEM((n_y - 1, u_dev, rank), F32),
        ]
        + [dma((n_z - 1,))] * 2
        + [dma((N_X - 1,))] * 2
        + [dma((N_X,))] * 2
        + [dma((n_y - 1,))] * 8,
        compiler_params=pltpu.CompilerParams(
            collective_id=0, has_side_effects=True, vmem_limit_bytes=48 * 2**20
        ),
        name="mttkrp_solve",
    )(
        user_index.reshape(groups, LANES),
        item_index.reshape(groups, LANES),
        week_index.reshape(groups, LANES),
        counts.astype(F32).reshape(groups, LANES),
        item_factor,
        week_factor,
    )


def solution(mesh):
    return jax.shard_map(
        functools.partial(local, mesh.shape["grid"], mesh.shape["slab"]),
        mesh=mesh,
        in_specs=(
            P(("grid", "slab")),
            P(("grid", "slab")),
            P(("grid", "slab")),
            P(("grid", "slab")),
            P(("grid", "slab"), None),
            P("slab", None),
        ),
        out_specs=P(("grid", "slab"), None),
        check_vma=False,
    )
```

```python
import functools

import jax
import jax.numpy as jnp
from jax import lax
from jax.experimental import pallas as pl
from jax.experimental.pallas import tpu as pltpu
from jax.sharding import PartitionSpec as P

MESH = pl.DeviceIdType.MESH
N_X = 4
N_CORE = 2
HI = 4
WEEK_HI = 2
LANES = 128
N_BLK = 2048
WEEK_BLK = 1024
PIVOTS = 4
PANEL = 32
F32 = jnp.float32
BF16 = jnp.bfloat16


def select_ones(row, table):
    h = table.shape[0]
    packed = jnp.broadcast_to(row, (16, LANES)).astype(jnp.int16)
    packed = jnp.concatenate([packed] * (h // 16), 0)
    return jnp.where(packed == table, BF16(1), BF16(0))


def dot_nt(a, b, **kw):
    return lax.dot_general(a, b, (((1,), (1,)), ((), ())), preferred_element_type=F32, **kw)


def dot_tn(a, b, **kw):
    return lax.dot_general(a, b, (((0,), (0,)), ((), ())), preferred_element_type=F32, **kw)


def invert_spd(a):
    n = a.shape[0]
    lane = lax.broadcasted_iota(jnp.int32, (PANEL, n), 1)
    sub = lax.broadcasted_iota(jnp.int32, (PANEL, n), 0)
    wide_lane = lax.broadcasted_iota(jnp.int32, (n, n), 1)
    m = PIVOTS

    def sweep(_, a):
        panel = a[:PANEL]
        x = panel
        for j in range(0, PANEL, m):
            cols = [jnp.broadcast_to(x[:, j + t : j + t + 1], (PANEL, n)) for t in range(m)]
            w = [[cols[t][j + r : j + r + 1] for t in range(m)] for r in range(m)]
            for p in range(m):
                inv = 1.0 / w[p][p]
                w[p] = [inv if t == p else w[p][t] * inv for t in range(m)]
                for r in range(m):
                    if r != p:
                        f = w[r][p]
                        w[r] = [-f * inv if t == p else w[r][t] - f * w[p][t] for t in range(m)]
            rows = []
            for r in range(m):
                row = w[r][0] * x[j : j + 1]
                for t in range(1, m):
                    row = row + w[r][t] * x[j + t : j + t + 1]
                for t in range(m):
                    row = jnp.where(lane[:1] == j + t, w[r][t], row)
                rows.append(row)
            x = jnp.where((lane >= j) & (lane < j + m), 0.0, x)
            for t in range(m):
                x = x - cols[t] * rows[t]
            for t in range(m):
                x = jnp.where(sub == j + t, jnp.broadcast_to(rows[t], (PANEL, n)), x)
        r = jnp.where(lane < PANEL, -x, x)
        rest = jnp.where(wide_lane < PANEL, 0.0, a) - dot_tn(panel, r, precision=lax.Precision.HIGHEST)
        a = jnp.concatenate([rest[PANEL:], r], 0)
        return pltpu.roll(a, n - PANEL, 1)

    return -lax.fori_loop(0, n // PANEL, sweep, a)


def kernel(
    n_z, n_y,
    user_hbm, item_ix_hbm, week_ix_hbm, count_hbm, item_hbm, week_hbm, out_ref,
    user_ref, item_ix_ref, week_ix_ref, count_in, item_ref, week_ref, count_ref,
    table, weeks, hot_item, hot_user, scaled, kr_all, tt, wt, iota, hi, lo,
    total, gram_part, gram_in, gram_all, rows_in,
    in_sem, z_send, z_recv, x_send, x_recv, c_send, c_recv, w_send, w_recv,
    g_send, g_recv, h_send, h_recv, m_send, m_recv,
):
    loads = []
    for k, (src, dst) in enumerate([
        (item_hbm, item_ref), (week_hbm, week_ref), (user_hbm, user_ref),
        (item_ix_hbm, item_ix_ref), (week_ix_hbm, week_ix_ref), (count_hbm, count_in),
    ]):
        copy = pltpu.make_async_copy(src, dst, in_sem.at[k])
        copy.start()
        loads.append(copy)
    g = lax.axis_index("grid")
    s = lax.axis_index("slab")
    z = g // (N_X * N_CORE)
    x = (g // N_CORE) % N_X
    c = g % N_CORE
    rank = item_ref.shape[1]
    per = item_ref.shape[0]
    groups = user_ref.shape[0]
    n_all = groups * LANES
    users = hot_user.shape[0]
    n_lo = hot_item.shape[0]
    n_week = weeks.shape[0] * weeks.shape[1]
    u_dev = out_ref.shape[0]

    def grid_id(zz, xx, cc):
        return (zz * N_X + xx) * N_CORE + cc

    def z_at(d):
        return lax.rem(z + d, n_z)

    def x_at(d):
        return lax.rem(x + d, N_X)

    def y_at(d):
        return lax.rem(s + d, n_y)

    z_peers = [(grid_id(z_at(d), x, c), s) for d in range(1, n_z)]
    x_peers = [(grid_id(z, x_at(d), c), s) for d in range(1, N_X)]
    c_peer = (grid_id(z, x, 1 - c), s)
    y_peers = [(g, y_at(d)) for d in range(1, n_y)]
    around = [(dx, dc) for dx in range(N_X) for dc in range(N_CORE) if dx or dc]

    def core_at(dc):
        return 1 - c if dc else c

    around_peers = [(grid_id(z, x_at(dx), core_at(dc)), s) for dx, dc in around]

    barrier = pltpu.get_barrier_semaphore()
    partners = around_peers + z_peers + y_peers
    for who in partners:
        pl.semaphore_signal(barrier, inc=1, device_id=who, device_id_type=MESH)

    iota[...] = lax.broadcasted_iota(jnp.int32, iota.shape, 0).astype(jnp.int16)
    for copy in loads:
        copy.wait()

    mid = n_z // 2
    l = item_ix_ref[...]
    grid_of = lax.shift_right_logical(l, per.bit_length() - 1)
    l_z = lax.shift_right_logical(grid_of, 3)
    l_x = lax.shift_right_logical(grid_of, 1) & 3
    hi[...] = (grid_of & 1) * 2 + lax.shift_right_logical(l_x, 1)
    l_slot = l_z + (mid - z)
    l_slot = jnp.where(l_slot < 0, l_slot + n_z, jnp.where(l_slot >= n_z, l_slot - n_z, l_slot))
    lo[...] = ((l_x & 1) * n_z + l_slot) * per + (l & (per - 1))
    user_ref[...] = (user_ref[...] + (n_y - lax.rem(s + 2, n_y)) * u_dev) & (users - 1)
    count_ref[...] = count_in[...].astype(F32)

    pl.semaphore_wait(barrier, len(partners))

    pending = []

    def send(src, dst, send_sem, recv_sem, who):
        copy = pltpu.make_async_remote_copy(
            src_ref=src, dst_ref=dst, send_sem=send_sem, recv_sem=recv_sem,
            device_id=who, device_id_type=MESH,
        )
        copy.start()
        pending.append(copy)

    def arrived(dst, send_sem, recv_sem, who):
        pltpu.make_async_remote_copy(
            src_ref=dst, dst_ref=dst, send_sem=send_sem, recv_sem=recv_sem,
            device_id=who, device_id_type=MESH,
        ).wait_recv()

    by_reach = sorted(range(1, n_z), key=lambda d: -min(d, n_z - d))
    for d in by_reach:
        send(item_ref, table.at[c, x, (mid - d) % n_z], z_send.at[d - 1], z_recv.at[d - 1], z_peers[d - 1])
    table[c, x, mid] = item_ref[...]
    far_y = sorted(range(1, n_y), key=lambda d: -min(d, n_y - d))
    for d in far_y:
        send(week_ref, weeks.at[s], w_send.at[d - 1], w_recv.at[d - 1], y_peers[d - 1])
    weeks[s] = week_ref[...]

    def make_user(r, carry):
        col = pl.ds(pl.multiple_of(r * LANES, LANES), LANES)
        hot_user[:, col] = select_ones(user_ref[pl.ds(r, 1), :], iota[:users])
        return carry

    def make_item(r, carry):
        col = pl.ds(pl.multiple_of(r * LANES, LANES), LANES)
        hot_item[:, col] = select_ones(lo[pl.ds(r, 1), :], iota[:n_lo])
        return carry

    far_x = sorted(range(1, N_X), key=lambda d: -min(d, N_X - d))

    def z_arrive(lo_reach, hi_reach):
        for reach in range(lo_reach, hi_reach + 1):
            for d in sorted({reach, n_z - reach}):
                arrived(table.at[c, x, (mid - d) % n_z], z_send.at[d - 1], z_recv.at[d - 1], z_peers[d - 1])

    def pass_on(first, count):
        part = table.at[c, x, pl.ds(first, count)]
        for d in far_x:
            copy = pltpu.make_async_remote_copy(
                src_ref=part, dst_ref=part, send_sem=x_send.at[d - 1], recv_sem=x_recv.at[d - 1],
                device_id=x_peers[d - 1], device_id_type=MESH,
            )
            copy.start()

    lax.fori_loop(0, groups, make_user, 0)
    near = min(2, mid - 1)
    wide = max(near, mid - 2)
    z_arrive(1, near)
    pass_on(mid - near, 2 * near + 1)
    lax.fori_loop(0, groups // 2, make_item, 0)
    if wide > near:
        z_arrive(near + 1, wide)
        pass_on(mid - wide, wide - near)
        pass_on(mid + near + 1, wide - near)
    lax.fori_loop(groups // 2, groups, make_item, 0)
    z_arrive(wide + 1, mid)
    pass_on(0, mid - wide)
    if n_z - (mid + wide + 1):
        pass_on(mid + wide + 1, n_z - (mid + wide + 1))
    send(table.at[c, x], table.at[c, x], c_send.at[0], c_recv.at[0], c_peer)

    eye = jnp.where(
        lax.broadcasted_iota(jnp.int32, (rank, rank), 0)
        == lax.broadcasted_iota(jnp.int32, (rank, rank), 1),
        1.0, 0.0,
    ).astype(BF16)

    for d in range(1, n_y):
        arrived(weeks.at[y_at(n_y - d)], w_send.at[d - 1], w_recv.at[d - 1], y_peers[d - 1])
    n_wlo = n_week // WEEK_HI
    for j in range(WEEK_HI):
        each = weeks.shape[0] // WEEK_HI
        part = weeks[j * each : (j + 1) * each].reshape(n_wlo, rank)
        wt[j * rank : (j + 1) * rank, :] = dot_nt(eye, part).astype(BF16)
    week_gram = dot_nt(wt[:rank], wt[:rank])
    for j in range(1, WEEK_HI):
        week_gram += dot_nt(wt[j * rank : (j + 1) * rank], wt[j * rank : (j + 1) * rank])

    per_week = WEEK_BLK // LANES

    def week_block(k, carry):
        hots = []
        for q in range(per_week):
            w = week_ix_ref[pl.ds(k * per_week + q, 1), :]
            hots.append(select_ones(w & (n_wlo - 1), iota[:n_wlo]))
        looked = jnp.dot(wt[...], jnp.concatenate(hots, 1), preferred_element_type=F32)
        for q in range(per_week):
            w = week_ix_ref[pl.ds(k * per_week + q, 1), :]
            top = jnp.broadcast_to(lax.shift_right_logical(w, n_wlo.bit_length() - 1), (rank, LANES))
            part = looked[:, q * LANES : (q + 1) * LANES]
            value = part[(WEEK_HI - 1) * rank :]
            for j in range(WEEK_HI - 2, -1, -1):
                value = jnp.where(top == j, part[j * rank : (j + 1) * rank], value)
            count = count_ref[pl.ds(k * per_week + q, 1), :]
            col = pl.ds(pl.multiple_of(k * WEEK_BLK + q * LANES, LANES), LANES)
            scaled[:, col] = value * count
        return carry

    lax.fori_loop(0, n_all // WEEK_BLK, week_block, 0)

    for d in range(1, N_X):
        spot = table.at[c, x_at(N_X - d)]
        arrived(spot, x_send.at[d - 1], x_recv.at[d - 1], x_peers[d - 1])
        send(spot, spot, c_send.at[d], c_recv.at[d], c_peer)

    half = N_X * N_CORE // HI

    def turn(core):
        sums = None
        for j in range(HI // N_CORE):
            part = table[core, j * half : (j + 1) * half].reshape(n_lo, rank)
            columns = dot_nt(eye, part).astype(BF16)
            tt[pl.ds(pl.multiple_of((core * (HI // N_CORE) + j) * rank, rank), rank), :] = columns
            term = dot_nt(columns, columns)
            sums = term if sums is None else sums + term
        return sums

    item_gram = turn(c)
    for d in range(N_X):
        spot = table.at[1 - c, x_at((N_X - d) % N_X)]
        arrived(spot, c_send.at[d], c_recv.at[d], c_peer)
    item_gram = item_gram + turn(1 - c)
    gram_part[...] = item_gram.reshape(gram_part.shape)
    e = x * N_CORE + c
    for d in far_y:
        send(gram_part.at[e], gram_in.at[d - 1], g_send.at[d - 1], g_recv.at[d - 1], y_peers[d - 1])

    per_blk = N_BLK // LANES

    def main_block(k, carry):
        col = pl.ds(pl.multiple_of(k * N_BLK, N_BLK), N_BLK)
        looked = jnp.dot(tt[...], hot_item[:, col], preferred_element_type=F32)
        kr = []
        for q in range(per_blk):
            top = jnp.broadcast_to(hi[pl.ds(k * per_blk + q, 1), :], (rank, LANES))
            part = looked[:, q * LANES : (q + 1) * LANES]
            value = part[(HI - 1) * rank :]
            for j in range(HI - 2, -1, -1):
                value = jnp.where(top == j, part[j * rank : (j + 1) * rank], value)
            at = pl.ds(pl.multiple_of(k * N_BLK + q * LANES, LANES), LANES)
            kr.append((value * scaled[:, at]).astype(BF16))
        kr_all[:, col] = jnp.concatenate(kr, 1)
        return carry

    blocks = n_all // N_BLK
    first = 3 * blocks // 4
    lax.fori_loop(0, first, main_block, 0)

    for d in range(1, n_y):
        arrived(gram_in.at[d - 1], g_send.at[d - 1], g_recv.at[d - 1], y_peers[d - 1])
    piece = gram_part[e]
    for d in range(1, n_y):
        piece = piece + gram_in[d - 1]
    gram_all[e] = piece
    for k in range(len(around)):
        send(gram_all.at[e], gram_all.at[e], h_send.at[k], h_recv.at[k], around_peers[k])

    lax.fori_loop(first, blocks, main_block, 0)

    half_users = users // 2
    for side in range(2):
        span = slice(side * half_users, (side + 1) * half_users)
        sums = dot_nt(hot_user[span, :], kr_all[...])
        mine = range(side * n_y // 2, (side + 1) * n_y // 2)
        total[side * n_y // 2 : (side + 1) * n_y // 2] = sums.reshape(n_y // 2, u_dev, rank)
        for d in far_y:
            if (d - 2) % n_y in mine:
                send(total.at[(d - 2) % n_y], rows_in.at[d - 1], m_send.at[d - 1], m_recv.at[d - 1], y_peers[d - 1])

    for k, (dx, dc) in enumerate(around):
        spot = gram_all.at[x_at((N_X - dx) % N_X) * N_CORE + core_at(dc)]
        arrived(spot, h_send.at[k], h_recv.at[k], around_peers[k])
    inverse = invert_spd(gram_all[...].reshape(rank, rank) * week_gram)

    for d in range(1, n_y):
        arrived(rows_in.at[d - 1], m_send.at[d - 1], m_recv.at[d - 1], y_peers[d - 1])
    rows = total[(0 - 2) % n_y]
    for d in range(1, n_y):
        rows = rows + rows_in[d - 1]
    out_ref[...] = jnp.dot(rows, inverse, preferred_element_type=F32, precision=lax.Precision.HIGHEST)

    for copy in pending:
        copy.wait_send()
    for d in range(1, N_X):
        slab = table.at[c, x]
        pltpu.make_async_remote_copy(
            src_ref=slab, dst_ref=slab, send_sem=x_send.at[d - 1], recv_sem=x_recv.at[d - 1],
            device_id=x_peers[d - 1], device_id_type=MESH,
        ).wait_send()


def local(n_grid, n_y, user_index, item_index, week_index, counts, item_factor, week_factor):
    n_all = user_index.shape[0]
    groups = n_all // LANES
    per, rank = item_factor.shape
    n_z = n_grid // (N_X * N_CORE)
    n_item = per * n_grid
    n_lo = n_item // HI
    n_week = week_factor.shape[0] * n_y
    u_dev = 64
    users = u_dev * n_y
    dma = pltpu.SemaphoreType.DMA
    return pl.pallas_call(
        functools.partial(kernel, n_z, n_y),
        out_shape=jax.ShapeDtypeStruct((u_dev, rank), F32),
        in_specs=[pl.BlockSpec(memory_space=pltpu.MemorySpace.HBM)] * 6,
        out_specs=pl.BlockSpec(memory_space=pltpu.VMEM),
        scratch_shapes=[
            pltpu.VMEM((groups, LANES), jnp.int32),
            pltpu.VMEM((groups, LANES), jnp.int32),
            pltpu.VMEM((groups, LANES), jnp.int32),
            pltpu.VMEM((groups, LANES), BF16),
            pltpu.VMEM(item_factor.shape, BF16),
            pltpu.VMEM(week_factor.shape, BF16),
            pltpu.VMEM((groups, LANES), F32),
            pltpu.VMEM((N_CORE, N_X, n_z, per, rank), BF16),
            pltpu.VMEM((n_y,) + week_factor.shape, BF16),
            pltpu.VMEM((n_lo, n_all), BF16),
            pltpu.VMEM((users, n_all), BF16),
            pltpu.VMEM((rank, n_all), F32),
            pltpu.VMEM((rank, n_all), BF16),
            pltpu.VMEM((HI * rank, n_lo), BF16),
            pltpu.VMEM((WEEK_HI * rank, n_week // WEEK_HI), BF16),
            pltpu.VMEM((max(n_lo, users), LANES), jnp.int16),
            pltpu.VMEM((groups, LANES), jnp.int32),
            pltpu.VMEM((groups, LANES), jnp.int32),
            pltpu.VMEM((n_y, u_dev, rank), F32),
            pltpu.VMEM((n_y, rank // n_y, rank), F32),
            pltpu.VMEM((n_y - 1, rank // n_y, rank), F32),
            pltpu.VMEM((n_y, rank // n_y, rank), F32),
            pltpu.VMEM((n_y - 1, u_dev, rank), F32),
        ]
        + [dma((6,))]
        + [dma((n_z - 1,))] * 2
        + [dma((N_X - 1,))] * 2
        + [dma((N_X,))] * 2
        + [dma((n_y - 1,))] * 8,
        compiler_params=pltpu.CompilerParams(
            collective_id=0, has_side_effects=True, vmem_limit_bytes=62914560
        ),
        name="mttkrp_solve",
    )(
        user_index.reshape(groups, LANES),
        item_index.reshape(groups, LANES),
        week_index.reshape(groups, LANES),
        counts.reshape(groups, LANES),
        item_factor,
        week_factor,
    )


def solution(mesh):
    return jax.shard_map(
        functools.partial(local, mesh.shape["grid"], mesh.shape["slab"]),
        mesh=mesh,
        in_specs=(
            P(("grid", "slab")),
            P(("grid", "slab")),
            P(("grid", "slab")),
            P(("grid", "slab")),
            P(("grid", "slab"), None),
            P("slab", None),
        ),
        out_specs=P(("grid", "slab"), None),
        check_vma=False,
    )
```

```python
import functools

import jax
import jax.numpy as jnp
from jax import lax
from jax.experimental import pallas as pl
from jax.experimental.pallas import tpu as pltpu
from jax.sharding import PartitionSpec as P

MESH = pl.DeviceIdType.MESH
N_X = 4
N_CORE = 2
HI = 4
WEEK_HI = 2
LANES = 128
N_BLK = 2048
WEEK_BLK = 1024
PIVOTS = 4
PANEL = 32
F32 = jnp.float32
BF16 = jnp.bfloat16


def select_ones(row, table):
    h = table.shape[0]
    packed = jnp.broadcast_to(row, (16, LANES)).astype(jnp.int16)
    packed = jnp.concatenate([packed] * (h // 16), 0)
    return jnp.where(packed == table, BF16(1), BF16(0))


def dot_nt(a, b, **kw):
    return lax.dot_general(a, b, (((1,), (1,)), ((), ())), preferred_element_type=F32, **kw)


def dot_tn(a, b, **kw):
    return lax.dot_general(a, b, (((0,), (0,)), ((), ())), preferred_element_type=F32, **kw)


def invert_spd(a):
    n = a.shape[0]
    lane = lax.broadcasted_iota(jnp.int32, (PANEL, n), 1)
    sub = lax.broadcasted_iota(jnp.int32, (PANEL, n), 0)
    wide_lane = lax.broadcasted_iota(jnp.int32, (n, n), 1)
    m = PIVOTS

    def sweep(_, a):
        panel = a[:PANEL]
        x = panel
        for j in range(0, PANEL, m):
            cols = [jnp.broadcast_to(x[:, j + t : j + t + 1], (PANEL, n)) for t in range(m)]
            w = [[cols[t][j + r : j + r + 1] for t in range(m)] for r in range(m)]
            for p in range(m):
                inv = 1.0 / w[p][p]
                w[p] = [inv if t == p else w[p][t] * inv for t in range(m)]
                for r in range(m):
                    if r != p:
                        f = w[r][p]
                        w[r] = [-f * inv if t == p else w[r][t] - f * w[p][t] for t in range(m)]
            rows = []
            for r in range(m):
                row = w[r][0] * x[j : j + 1]
                for t in range(1, m):
                    row = row + w[r][t] * x[j + t : j + t + 1]
                for t in range(m):
                    row = jnp.where(lane[:1] == j + t, w[r][t], row)
                rows.append(row)
            x = jnp.where((lane >= j) & (lane < j + m), 0.0, x)
            for t in range(m):
                x = x - cols[t] * rows[t]
            for t in range(m):
                x = jnp.where(sub == j + t, jnp.broadcast_to(rows[t], (PANEL, n)), x)
        r = jnp.where(lane < PANEL, -x, x)
        rest = jnp.where(wide_lane < PANEL, 0.0, a) - dot_tn(panel, r, precision=lax.Precision.HIGHEST)
        a = jnp.concatenate([rest[PANEL:], r], 0)
        return pltpu.roll(a, n - PANEL, 1)

    return -lax.fori_loop(0, n // PANEL, sweep, a)


def kernel(
    n_z, n_y,
    user_hbm, item_ix_hbm, week_ix_hbm, count_hbm, item_hbm, week_hbm, out_ref,
    user_ref, item_ix_ref, week_ix_ref, count_in, item_ref, week_ref, count_ref,
    table, weeks, hot_item, hot_user, scaled, kr_all, tt, wt, iota, hi, lo,
    total, gram_part, gram_in, gram_all, rows_in,
    in_sem, z_send, z_recv, x_send, x_recv, c_send, c_recv, w_send, w_recv,
    g_send, g_recv, h_send, h_recv, m_send, m_recv,
):
    loads = []
    for k, (src, dst) in enumerate([
        (item_hbm, item_ref), (week_hbm, week_ref), (user_hbm, user_ref),
        (item_ix_hbm, item_ix_ref), (week_ix_hbm, week_ix_ref), (count_hbm, count_in),
    ]):
        copy = pltpu.make_async_copy(src, dst, in_sem.at[k])
        copy.start()
        loads.append(copy)
    g = lax.axis_index("grid")
    s = lax.axis_index("slab")
    z = g // (N_X * N_CORE)
    x = (g // N_CORE) % N_X
    c = g % N_CORE
    rank = item_ref.shape[1]
    per = item_ref.shape[0]
    groups = user_ref.shape[0]
    n_all = groups * LANES
    users = hot_user.shape[0]
    n_lo = hot_item.shape[0]
    n_week = weeks.shape[0] * weeks.shape[1]
    u_dev = out_ref.shape[0]

    def grid_id(zz, xx, cc):
        return (zz * N_X + xx) * N_CORE + cc

    def z_at(d):
        return lax.rem(z + d, n_z)

    def x_at(d):
        return lax.rem(x + d, N_X)

    def y_at(d):
        return lax.rem(s + d, n_y)

    z_peers = [(grid_id(z_at(d), x, c), s) for d in range(1, n_z)]
    x_peers = [(grid_id(z, x_at(d), c), s) for d in range(1, N_X)]
    c_peer = (grid_id(z, x, 1 - c), s)
    y_peers = [(g, y_at(d)) for d in range(1, n_y)]
    around = [(dx, dc) for dx in range(N_X) for dc in range(N_CORE) if dx or dc]

    def core_at(dc):
        return 1 - c if dc else c

    around_peers = [(grid_id(z, x_at(dx), core_at(dc)), s) for dx, dc in around]

    barrier = pltpu.get_barrier_semaphore()
    by_reach = sorted(range(1, n_z), key=lambda d: -min(d, n_z - d))
    far_y = sorted(range(1, n_y), key=lambda d: -min(d, n_y - d))
    partners = [z_peers[d - 1] for d in by_reach] + [y_peers[d - 1] for d in far_y] + around_peers
    for who in partners:
        pl.semaphore_signal(barrier, inc=1, device_id=who, device_id_type=MESH)

    loads[0].wait()
    loads[1].wait()
    pl.semaphore_wait(barrier, len(partners))

    mid = n_z // 2
    pending = []

    def send(src, dst, send_sem, recv_sem, who):
        copy = pltpu.make_async_remote_copy(
            src_ref=src, dst_ref=dst, send_sem=send_sem, recv_sem=recv_sem,
            device_id=who, device_id_type=MESH,
        )
        copy.start()
        pending.append(copy)

    def arrived(dst, send_sem, recv_sem, who):
        pltpu.make_async_remote_copy(
            src_ref=dst, dst_ref=dst, send_sem=send_sem, recv_sem=recv_sem,
            device_id=who, device_id_type=MESH,
        ).wait_recv()

    for d in by_reach:
        send(item_ref, table.at[c, x, (mid - d) % n_z], z_send.at[d - 1], z_recv.at[d - 1], z_peers[d - 1])
    table[c, x, mid] = item_ref[...]
    for d in far_y:
        send(week_ref, weeks.at[s], w_send.at[d - 1], w_recv.at[d - 1], y_peers[d - 1])
    weeks[s] = week_ref[...]

    iota[...] = lax.broadcasted_iota(jnp.int32, iota.shape, 0).astype(jnp.int16)
    for copy in loads[2:]:
        copy.wait()

    l = item_ix_ref[...]
    grid_of = lax.shift_right_logical(l, per.bit_length() - 1)
    l_z = lax.shift_right_logical(grid_of, 3)
    l_x = lax.shift_right_logical(grid_of, 1) & 3
    hi[...] = ((grid_of & 1) ^ c) * 2 + lax.shift_right_logical(l_x, 1)
    l_slot = l_z + (mid - z)
    l_slot = jnp.where(l_slot < 0, l_slot + n_z, jnp.where(l_slot >= n_z, l_slot - n_z, l_slot))
    lo[...] = ((l_x & 1) * n_z + l_slot) * per + (l & (per - 1))
    user_ref[...] = (user_ref[...] + (n_y - lax.rem(s + 2, n_y)) * u_dev) & (users - 1)
    count_ref[...] = count_in[...].astype(F32)

    def make_user(r, carry):
        col = pl.ds(pl.multiple_of(r * LANES, LANES), LANES)
        hot_user[:, col] = select_ones(user_ref[pl.ds(r, 1), :], iota[:users])
        return carry

    def make_item(r, carry):
        col = pl.ds(pl.multiple_of(r * LANES, LANES), LANES)
        hot_item[:, col] = select_ones(lo[pl.ds(r, 1), :], iota[:n_lo])
        return carry

    far_x = sorted(range(1, N_X), key=lambda d: -min(d, N_X - d))

    def z_arrive(lo_reach, hi_reach):
        for reach in range(lo_reach, hi_reach + 1):
            for d in sorted({reach, n_z - reach}):
                arrived(table.at[c, x, (mid - d) % n_z], z_send.at[d - 1], z_recv.at[d - 1], z_peers[d - 1])

    def pass_on(first, count):
        part = table.at[c, x, pl.ds(first, count)]
        for d in far_x:
            copy = pltpu.make_async_remote_copy(
                src_ref=part, dst_ref=part, send_sem=x_send.at[d - 1], recv_sem=x_recv.at[d - 1],
                device_id=x_peers[d - 1], device_id_type=MESH,
            )
            copy.start()

    lax.fori_loop(0, groups, make_user, 0)
    near = min(2, mid - 1)
    wide = max(near, mid - 2)
    z_arrive(1, near)
    pass_on(mid - near, 2 * near + 1)
    lax.fori_loop(0, groups // 2, make_item, 0)
    if wide > near:
        z_arrive(near + 1, wide)
        pass_on(mid - wide, wide - near)
        pass_on(mid + near + 1, wide - near)
    lax.fori_loop(groups // 2, groups, make_item, 0)
    z_arrive(wide + 1, mid)
    pass_on(0, mid - wide)
    if n_z - (mid + wide + 1):
        pass_on(mid + wide + 1, n_z - (mid + wide + 1))
    send(table.at[c, x], table.at[c, x], c_send.at[0], c_recv.at[0], c_peer)

    eye = jnp.where(
        lax.broadcasted_iota(jnp.int32, (rank, rank), 0)
        == lax.broadcasted_iota(jnp.int32, (rank, rank), 1),
        1.0, 0.0,
    ).astype(BF16)

    for d in range(1, n_y):
        arrived(weeks.at[y_at(n_y - d)], w_send.at[d - 1], w_recv.at[d - 1], y_peers[d - 1])
    n_wlo = n_week // WEEK_HI
    for j in range(WEEK_HI):
        each = weeks.shape[0] // WEEK_HI
        part = weeks[j * each : (j + 1) * each].reshape(n_wlo, rank)
        wt[j * rank : (j + 1) * rank, :] = dot_nt(eye, part).astype(BF16)
    week_gram = dot_nt(wt[:rank], wt[:rank])
    for j in range(1, WEEK_HI):
        week_gram += dot_nt(wt[j * rank : (j + 1) * rank], wt[j * rank : (j + 1) * rank])

    per_week = WEEK_BLK // LANES

    def week_block(k, carry):
        hots = []
        for q in range(per_week):
            w = week_ix_ref[pl.ds(k * per_week + q, 1), :]
            hots.append(select_ones(w & (n_wlo - 1), iota[:n_wlo]))
        looked = jnp.dot(wt[...], jnp.concatenate(hots, 1), preferred_element_type=F32)
        for q in range(per_week):
            w = week_ix_ref[pl.ds(k * per_week + q, 1), :]
            top = jnp.broadcast_to(lax.shift_right_logical(w, n_wlo.bit_length() - 1), (rank, LANES))
            part = looked[:, q * LANES : (q + 1) * LANES]
            value = part[(WEEK_HI - 1) * rank :]
            for j in range(WEEK_HI - 2, -1, -1):
                value = jnp.where(top == j, part[j * rank : (j + 1) * rank], value)
            count = count_ref[pl.ds(k * per_week + q, 1), :]
            col = pl.ds(pl.multiple_of(k * WEEK_BLK + q * LANES, LANES), LANES)
            scaled[:, col] = value * count
        return carry

    lax.fori_loop(0, n_all // WEEK_BLK, week_block, 0)

    for d in range(1, N_X):
        spot = table.at[c, x_at(N_X - d)]
        arrived(spot, x_send.at[d - 1], x_recv.at[d - 1], x_peers[d - 1])
        send(spot, spot, c_send.at[d], c_recv.at[d], c_peer)

    half = N_X * N_CORE // HI

    def turn(core):
        rows = pl.ds(pl.multiple_of(core * own * rank, own * rank), own * rank)
        tt[rows, :] = jnp.concatenate(
            [
                dot_nt(eye, table[core, j * half : (j + 1) * half].reshape(n_lo, rank)).astype(BF16)
                for j in range(own)
            ],
            0,
        )
        return rows

    own = HI // N_CORE
    mine = turn(c)
    own_gram = None
    for j in range(own):
        columns = tt[pl.ds(pl.multiple_of((c * own + j) * rank, rank), rank), :]
        term = dot_nt(columns, columns)
        own_gram = term if own_gram is None else own_gram + term
    gram_part[...] = own_gram.reshape(gram_part.shape)
    for d in far_y:
        send(gram_part.at[x], gram_in.at[d - 1], g_send.at[d - 1], g_recv.at[d - 1], y_peers[d - 1])

    per_blk = N_BLK // LANES
    blocks = n_all // N_BLK

    def look_up(rows, k, finish):
        col = pl.ds(pl.multiple_of(k * N_BLK, N_BLK), N_BLK)
        looked = jnp.dot(tt[rows, :], hot_item[:, col], preferred_element_type=F32)
        parts = []
        for q in range(per_blk):
            part = looked[:, q * LANES : (q + 1) * LANES]
            top = jnp.broadcast_to(hi[pl.ds(k * per_blk + q, 1), :], (rank, LANES))
            parts.append(finish(k, q, top, part[:rank], part[rank:]))
        kr_all[:, col] = jnp.concatenate(parts, 1)

    def pick_own(k, carry):
        look_up(mine, k, lambda k, q, top, low, high: jnp.where(top == 0, low, high).astype(BF16))
        return carry

    def finish_other(k, q, top, low, high):
        at = pl.ds(pl.multiple_of(k * N_BLK + q * LANES, LANES), LANES)
        value = jnp.where(top < 2, kr_all[:, at].astype(F32), jnp.where(top == 2, low, high))
        return (value * scaled[:, at]).astype(BF16)

    def add_users(k, span):
        col = pl.ds(pl.multiple_of(k * N_BLK, N_BLK), N_BLK)
        sums = dot_nt(hot_user[span.start * u_dev : span.stop * u_dev, col], kr_all[:, col])
        total[span] += sums.reshape(span.stop - span.start, u_dev, rank)

    def pick_other(k, carry):
        look_up(other, k, finish_other)
        add_users(k, slice(0, n_y))
        return carry

    total[...] = jnp.zeros_like(total)
    lax.fori_loop(0, blocks, pick_own, 0)

    for d in range(N_X):
        spot = table.at[1 - c, x_at((N_X - d) % N_X)]
        arrived(spot, c_send.at[d], c_recv.at[d], c_peer)
    other = turn(1 - c)

    lax.fori_loop(0, blocks // 2, pick_other, 0)

    for d in range(1, n_y):
        arrived(gram_in.at[d - 1], g_send.at[d - 1], g_recv.at[d - 1], y_peers[d - 1])
    piece = gram_part[x]
    for d in range(1, n_y):
        piece = piece + gram_in[d - 1]
    gram_all[c, x] = piece
    for k in range(len(around)):
        send(gram_all.at[c, x], gram_all.at[c, x], h_send.at[k], h_recv.at[k], around_peers[k])

    lax.fori_loop(blocks // 2, blocks - 1, pick_other, 0)
    look_up(other, blocks - 1, finish_other)
    for side in range(2):
        held = range(side * n_y // 2, (side + 1) * n_y // 2)
        add_users(blocks - 1, slice(held.start, held.stop))
        for d in far_y:
            if (d - 2) % n_y in held:
                send(total.at[(d - 2) % n_y], rows_in.at[d - 1], m_send.at[d - 1], m_recv.at[d - 1], y_peers[d - 1])

    for k, (dx, dc) in enumerate(around):
        spot = gram_all.at[core_at(dc), x_at((N_X - dx) % N_X)]
        arrived(spot, h_send.at[k], h_recv.at[k], around_peers[k])
    item_gram = gram_all[0]
    for core in range(1, N_CORE):
        item_gram = item_gram + gram_all[core]
    inverse = invert_spd(item_gram.reshape(rank, rank) * week_gram)

    for d in range(1, n_y):
        arrived(rows_in.at[d - 1], m_send.at[d - 1], m_recv.at[d - 1], y_peers[d - 1])
    rows = total[(0 - 2) % n_y]
    for d in range(1, n_y):
        rows = rows + rows_in[d - 1]
    out_ref[...] = jnp.dot(rows, inverse, preferred_element_type=F32, precision=lax.Precision.HIGHEST)

    for copy in pending:
        copy.wait_send()
    for d in range(1, N_X):
        slab = table.at[c, x]
        pltpu.make_async_remote_copy(
            src_ref=slab, dst_ref=slab, send_sem=x_send.at[d - 1], recv_sem=x_recv.at[d - 1],
            device_id=x_peers[d - 1], device_id_type=MESH,
        ).wait_send()


def local(n_grid, n_y, user_index, item_index, week_index, counts, item_factor, week_factor):
    n_all = user_index.shape[0]
    groups = n_all // LANES
    per, rank = item_factor.shape
    n_z = n_grid // (N_X * N_CORE)
    n_item = per * n_grid
    n_lo = n_item // HI
    n_week = week_factor.shape[0] * n_y
    u_dev = 64
    users = u_dev * n_y
    dma = pltpu.SemaphoreType.DMA
    return pl.pallas_call(
        functools.partial(kernel, n_z, n_y),
        out_shape=jax.ShapeDtypeStruct((u_dev, rank), F32),
        in_specs=[pl.BlockSpec(memory_space=pltpu.MemorySpace.HBM)] * 6,
        out_specs=pl.BlockSpec(memory_space=pltpu.VMEM),
        scratch_shapes=[
            pltpu.VMEM((groups, LANES), jnp.int32),
            pltpu.VMEM((groups, LANES), jnp.int32),
            pltpu.VMEM((groups, LANES), jnp.int32),
            pltpu.VMEM((groups, LANES), BF16),
            pltpu.VMEM(item_factor.shape, BF16),
            pltpu.VMEM(week_factor.shape, BF16),
            pltpu.VMEM((groups, LANES), F32),
            pltpu.VMEM((N_CORE, N_X, n_z, per, rank), BF16),
            pltpu.VMEM((n_y,) + week_factor.shape, BF16),
            pltpu.VMEM((n_lo, n_all), BF16),
            pltpu.VMEM((users, n_all), BF16),
            pltpu.VMEM((rank, n_all), F32),
            pltpu.VMEM((rank, n_all), BF16),
            pltpu.VMEM((HI * rank, n_lo), BF16),
            pltpu.VMEM((WEEK_HI * rank, n_week // WEEK_HI), BF16),
            pltpu.VMEM((max(n_lo, users), LANES), jnp.int16),
            pltpu.VMEM((groups, LANES), jnp.int32),
            pltpu.VMEM((groups, LANES), jnp.int32),
            pltpu.VMEM((n_y, u_dev, rank), F32),
            pltpu.VMEM((N_X, rank // N_X, rank), F32),
            pltpu.VMEM((n_y - 1, rank // N_X, rank), F32),
            pltpu.VMEM((N_CORE, N_X, rank // N_X, rank), F32),
            pltpu.VMEM((n_y - 1, u_dev, rank), F32),
        ]
        + [dma((6,))]
        + [dma((n_z - 1,))] * 2
        + [dma((N_X - 1,))] * 2
        + [dma((N_X,))] * 2
        + [dma((n_y - 1,))] * 4
        + [dma((N_X * N_CORE - 1,))] * 2
        + [dma((n_y - 1,))] * 2,
        compiler_params=pltpu.CompilerParams(
            collective_id=0, has_side_effects=True, vmem_limit_bytes=62914560
        ),
        name="mttkrp_solve",
    )(
        user_index.reshape(groups, LANES),
        item_index.reshape(groups, LANES),
        week_index.reshape(groups, LANES),
        counts.reshape(groups, LANES),
        item_factor,
        week_factor,
    )


def solution(mesh):
    return jax.shard_map(
        functools.partial(local, mesh.shape["grid"], mesh.shape["slab"]),
        mesh=mesh,
        in_specs=(
            P(("grid", "slab")),
            P(("grid", "slab")),
            P(("grid", "slab")),
            P(("grid", "slab")),
            P(("grid", "slab"), None),
            P("slab", None),
        ),
        out_specs=P(("grid", "slab"), None),
        check_vma=False,
    )
```

```python
import functools

import jax
import jax.numpy as jnp
from jax import lax
from jax.experimental import pallas as pl
from jax.experimental.pallas import tpu as pltpu
from jax.sharding import PartitionSpec as P

MESH = pl.DeviceIdType.MESH
N_X = 4
N_CORE = 2
HI = 4
WEEK_HI = 2
LANES = 128
N_BLK = 2048
WEEK_BLK = 1024
PIVOTS = 4
PANEL = 32
F32 = jnp.float32
BF16 = jnp.bfloat16


def select_ones(row, table):
    h = table.shape[0]
    packed = jnp.broadcast_to(row, (16, LANES)).astype(jnp.int16)
    packed = jnp.concatenate([packed] * (h // 16), 0)
    return jnp.where(packed == table, BF16(1), BF16(0))


def dot_nt(a, b, **kw):
    return lax.dot_general(a, b, (((1,), (1,)), ((), ())), preferred_element_type=F32, **kw)


def dot_tn(a, b, **kw):
    return lax.dot_general(a, b, (((0,), (0,)), ((), ())), preferred_element_type=F32, **kw)


def invert_spd(a):
    n = a.shape[0]
    lane = lax.broadcasted_iota(jnp.int32, (PANEL, n), 1)
    sub = lax.broadcasted_iota(jnp.int32, (PANEL, n), 0)
    wide_lane = lax.broadcasted_iota(jnp.int32, (n, n), 1)
    m = PIVOTS

    def sweep(_, a):
        panel = a[:PANEL]
        x = panel
        for j in range(0, PANEL, m):
            cols = [jnp.broadcast_to(x[:, j + t : j + t + 1], (PANEL, n)) for t in range(m)]
            w = [[cols[t][j + r : j + r + 1] for t in range(m)] for r in range(m)]
            for p in range(m):
                inv = 1.0 / w[p][p]
                w[p] = [inv if t == p else w[p][t] * inv for t in range(m)]
                for r in range(m):
                    if r != p:
                        f = w[r][p]
                        w[r] = [-f * inv if t == p else w[r][t] - f * w[p][t] for t in range(m)]
            rows = []
            for r in range(m):
                row = w[r][0] * x[j : j + 1]
                for t in range(1, m):
                    row = row + w[r][t] * x[j + t : j + t + 1]
                for t in range(m):
                    row = jnp.where(lane[:1] == j + t, w[r][t], row)
                rows.append(row)
            x = jnp.where((lane >= j) & (lane < j + m), 0.0, x)
            for t in range(m):
                x = x - cols[t] * rows[t]
            for t in range(m):
                x = jnp.where(sub == j + t, jnp.broadcast_to(rows[t], (PANEL, n)), x)
        r = jnp.where(lane < PANEL, -x, x)
        rest = jnp.where(wide_lane < PANEL, 0.0, a) - dot_tn(panel, r, precision=lax.Precision.HIGHEST)
        a = jnp.concatenate([rest[PANEL:], r], 0)
        return pltpu.roll(a, n - PANEL, 1)

    return -lax.fori_loop(0, n // PANEL, sweep, a)


def kernel(
    n_z, n_y,
    user_hbm, item_ix_hbm, week_ix_hbm, count_hbm, item_hbm, week_hbm, out_ref,
    user_ref, item_ix_ref, week_ix_ref, count_in, item_ref, week_ref, count_ref,
    table, weeks, hot_item, hot_user, scaled, kr_all, tt, wt, iota, hi, lo,
    total, gram_part, gram_in, gram_all, rows_in,
    in_sem, z_send, z_recv, x_send, x_recv, c_send, c_recv, w_send, w_recv,
    g_send, g_recv, h_send, h_recv, m_send, m_recv,
):
    loads = []
    for k, (src, dst) in enumerate([
        (item_hbm, item_ref), (week_hbm, week_ref), (user_hbm, user_ref),
        (item_ix_hbm, item_ix_ref), (week_ix_hbm, week_ix_ref), (count_hbm, count_in),
    ]):
        copy = pltpu.make_async_copy(src, dst, in_sem.at[k])
        copy.start()
        loads.append(copy)
    g = lax.axis_index("grid")
    s = lax.axis_index("slab")
    z = g // (N_X * N_CORE)
    x = (g // N_CORE) % N_X
    c = g % N_CORE
    rank = item_ref.shape[1]
    per = item_ref.shape[0]
    groups = user_ref.shape[0]
    n_all = groups * LANES
    users = hot_user.shape[0]
    n_lo = hot_item.shape[0]
    n_week = weeks.shape[0] * weeks.shape[1]
    u_dev = out_ref.shape[0]

    def grid_id(zz, xx, cc):
        return (zz * N_X + xx) * N_CORE + cc

    def z_at(d):
        return lax.rem(z + d, n_z)

    def x_at(d):
        return lax.rem(x + d, N_X)

    def y_at(d):
        return lax.rem(s + d, n_y)

    z_peers = [(grid_id(z_at(d), x, c), s) for d in range(1, n_z)]
    x_peers = [(grid_id(z, x_at(d), c), s) for d in range(1, N_X)]
    c_peer = (grid_id(z, x, 1 - c), s)
    y_peers = [(g, y_at(d)) for d in range(1, n_y)]
    around = [(dx, dc) for dx in range(N_X) for dc in range(N_CORE) if dx or dc]

    def core_at(dc):
        return 1 - c if dc else c

    around_peers = [(grid_id(z, x_at(dx), core_at(dc)), s) for dx, dc in around]

    barrier = pltpu.get_barrier_semaphore()
    by_reach = sorted(range(1, n_z), key=lambda d: -min(d, n_z - d))
    far_y = sorted(range(1, n_y), key=lambda d: -min(d, n_y - d))
    partners = [z_peers[d - 1] for d in by_reach] + [y_peers[d - 1] for d in far_y] + around_peers
    for who in partners:
        pl.semaphore_signal(barrier, inc=1, device_id=who, device_id_type=MESH)

    loads[0].wait()
    loads[1].wait()
    pl.semaphore_wait(barrier, len(partners))

    mid = n_z // 2
    pending = []

    def send(src, dst, send_sem, recv_sem, who):
        copy = pltpu.make_async_remote_copy(
            src_ref=src, dst_ref=dst, send_sem=send_sem, recv_sem=recv_sem,
            device_id=who, device_id_type=MESH,
        )
        copy.start()
        pending.append(copy)

    def arrived(dst, send_sem, recv_sem, who):
        pltpu.make_async_remote_copy(
            src_ref=dst, dst_ref=dst, send_sem=send_sem, recv_sem=recv_sem,
            device_id=who, device_id_type=MESH,
        ).wait_recv()

    for d in by_reach:
        send(item_ref, table.at[c, 0, (mid - d) % n_z], z_send.at[d - 1], z_recv.at[d - 1], z_peers[d - 1])
    table[c, 0, mid] = item_ref[...]
    for d in far_y:
        send(week_ref, weeks.at[s], w_send.at[d - 1], w_recv.at[d - 1], y_peers[d - 1])
    weeks[s] = week_ref[...]

    iota[...] = lax.broadcasted_iota(jnp.int32, iota.shape, 0).astype(jnp.int16)
    for copy in loads[2:]:
        copy.wait()

    l = item_ix_ref[...]
    grid_of = lax.shift_right_logical(l, per.bit_length() - 1)
    l_z = lax.shift_right_logical(grid_of, 3)
    l_x = (lax.shift_right_logical(grid_of, 1) + (N_X - x)) & 3
    hi[...] = ((grid_of & 1) ^ c) * 2 + lax.shift_right_logical(l_x, 1)
    l_slot = l_z + (mid - z)
    l_slot = jnp.where(l_slot < 0, l_slot + n_z, jnp.where(l_slot >= n_z, l_slot - n_z, l_slot))
    lo[...] = ((l_x & 1) * n_z + l_slot) * per + (l & (per - 1))
    user_ref[...] = (user_ref[...] + (n_y - lax.rem(s + 2, n_y)) * u_dev) & (users - 1)
    count_ref[...] = count_in[...].astype(F32)

    def make_user(r, carry):
        col = pl.ds(pl.multiple_of(r * LANES, LANES), LANES)
        hot_user[:, col] = select_ones(user_ref[pl.ds(r, 1), :], iota[:users])
        return carry

    def make_item(r, carry):
        col = pl.ds(pl.multiple_of(r * LANES, LANES), LANES)
        hot_item[:, col] = select_ones(lo[pl.ds(r, 1), :], iota[:n_lo])
        return carry

    far_x = sorted(range(1, N_X), key=lambda d: -min(d, N_X - d))

    def z_arrive(lo_reach, hi_reach):
        for reach in range(lo_reach, hi_reach + 1):
            for d in sorted({reach, n_z - reach}):
                arrived(table.at[c, 0, (mid - d) % n_z], z_send.at[d - 1], z_recv.at[d - 1], z_peers[d - 1])

    def pass_on(first, count):
        part = table.at[c, 0, pl.ds(first, count)]
        for d in far_x:
            copy = pltpu.make_async_remote_copy(
                src_ref=part, dst_ref=table.at[c, N_X - d, pl.ds(first, count)], send_sem=x_send.at[d - 1], recv_sem=x_recv.at[d - 1],
                device_id=x_peers[d - 1], device_id_type=MESH,
            )
            copy.start()

    lax.fori_loop(0, groups, make_user, 0)
    near = min(2, mid - 1)
    wide = max(near, mid - 2)
    z_arrive(1, near)
    pass_on(mid - near, 2 * near + 1)
    lax.fori_loop(0, groups // 2, make_item, 0)
    if wide > near:
        z_arrive(near + 1, wide)
        pass_on(mid - wide, wide - near)
        pass_on(mid + near + 1, wide - near)
    lax.fori_loop(groups // 2, groups, make_item, 0)
    z_arrive(wide + 1, mid)
    pass_on(0, mid - wide)
    if n_z - (mid + wide + 1):
        pass_on(mid + wide + 1, n_z - (mid + wide + 1))
    send(table.at[c, 0], table.at[c, 0], c_send.at[0], c_recv.at[0], c_peer)

    eye = jnp.where(
        lax.broadcasted_iota(jnp.int32, (rank, rank), 0)
        == lax.broadcasted_iota(jnp.int32, (rank, rank), 1),
        1.0, 0.0,
    ).astype(BF16)

    for d in range(1, n_y):
        arrived(weeks.at[y_at(n_y - d)], w_send.at[d - 1], w_recv.at[d - 1], y_peers[d - 1])
    n_wlo = n_week // WEEK_HI
    for j in range(WEEK_HI):
        each = weeks.shape[0] // WEEK_HI
        part = weeks[j * each : (j + 1) * each].reshape(n_wlo, rank)
        wt[j * rank : (j + 1) * rank, :] = dot_nt(eye, part).astype(BF16)
    week_gram = dot_nt(wt[:rank], wt[:rank])
    for j in range(1, WEEK_HI):
        week_gram += dot_nt(wt[j * rank : (j + 1) * rank], wt[j * rank : (j + 1) * rank])

    per_week = WEEK_BLK // LANES

    def week_block(k, carry):
        hots = []
        for q in range(per_week):
            w = week_ix_ref[pl.ds(k * per_week + q, 1), :]
            hots.append(select_ones(w & (n_wlo - 1), iota[:n_wlo]))
        looked = jnp.dot(wt[...], jnp.concatenate(hots, 1), preferred_element_type=F32)
        for q in range(per_week):
            w = week_ix_ref[pl.ds(k * per_week + q, 1), :]
            top = jnp.broadcast_to(lax.shift_right_logical(w, n_wlo.bit_length() - 1), (rank, LANES))
            part = looked[:, q * LANES : (q + 1) * LANES]
            value = part[(WEEK_HI - 1) * rank :]
            for j in range(WEEK_HI - 2, -1, -1):
                value = jnp.where(top == j, part[j * rank : (j + 1) * rank], value)
            count = count_ref[pl.ds(k * per_week + q, 1), :]
            col = pl.ds(pl.multiple_of(k * WEEK_BLK + q * LANES, LANES), LANES)
            scaled[:, col] = value * count
        return carry

    lax.fori_loop(0, n_all // WEEK_BLK, week_block, 0)

    def x_arrive(d):
        spot = table.at[c, N_X - d]
        arrived(spot, x_send.at[d - 1], x_recv.at[d - 1], x_peers[d - 1])
        send(spot, spot, c_send.at[d], c_recv.at[d], c_peer)

    half = N_X * N_CORE // HI

    own = HI // N_CORE

    def turn(core, j):
        rows = pl.ds(pl.multiple_of((core * own + j) * rank, rank), rank)
        tt[rows, :] = dot_nt(eye, table[core, j * half : (j + 1) * half].reshape(n_lo, rank)).astype(BF16)
        return rows

    per_blk = N_BLK // LANES
    blocks = n_all // N_BLK

    def look_up(rows, k, finish):
        col = pl.ds(pl.multiple_of(k * N_BLK, N_BLK), N_BLK)
        looked = jnp.dot(tt[rows, :], hot_item[:, col], preferred_element_type=F32)
        parts = []
        for q in range(per_blk):
            part = looked[:, q * LANES : (q + 1) * LANES]
            top = jnp.broadcast_to(hi[pl.ds(k * per_blk + q, 1), :], (rank, LANES))
            parts.append(finish(k, q, top, part[:rank], part[-rank:]))
        kr_all[:, col] = jnp.concatenate(parts, 1)

    def pick_first(k, carry):
        look_up(first_rows, k, lambda k, q, top, low, high: low.astype(BF16))
        return carry

    def finish_second(k, q, top, low, high):
        at = pl.ds(pl.multiple_of(k * N_BLK + q * LANES, LANES), LANES)
        return jnp.where(top == 0, kr_all[:, at].astype(F32), low).astype(BF16)

    def pick_second(k, carry):
        look_up(second_rows, k, finish_second)
        return carry

    def finish_other(k, q, top, low, high):
        at = pl.ds(pl.multiple_of(k * N_BLK + q * LANES, LANES), LANES)
        value = jnp.where(top < 2, kr_all[:, at].astype(F32), jnp.where(top == 2, low, high))
        return (value * scaled[:, at]).astype(BF16)

    def add_users(k, span):
        col = pl.ds(pl.multiple_of(k * N_BLK, N_BLK), N_BLK)
        sums = dot_nt(hot_user[span.start * u_dev : span.stop * u_dev, col], kr_all[:, col])
        total[span] += sums.reshape(span.stop - span.start, u_dev, rank)

    def pick_other(k, carry):
        look_up(other, k, finish_other)
        add_users(k, slice(0, n_y))
        return carry

    total[...] = jnp.zeros_like(total)
    x_arrive(N_X - 1)
    first_rows = turn(c, 0)
    lax.fori_loop(0, blocks, pick_first, 0)
    for d in range(1, N_X - 1):
        x_arrive(d)
    second_rows = turn(c, 1)
    own_gram = None
    for j in range(own):
        columns = tt[pl.ds(pl.multiple_of((c * own + j) * rank, rank), rank), :]
        term = dot_nt(columns, columns)
        own_gram = term if own_gram is None else own_gram + term
    gram_part[...] = own_gram.reshape(gram_part.shape)
    for d in far_y:
        send(gram_part.at[x], gram_in.at[d - 1], g_send.at[d - 1], g_recv.at[d - 1], y_peers[d - 1])

    lax.fori_loop(0, blocks, pick_second, 0)

    for d in range(N_X):
        spot = table.at[1 - c, (N_X - d) % N_X]
        arrived(spot, c_send.at[d], c_recv.at[d], c_peer)
    for j in range(own):
        turn(1 - c, j)
    other = pl.ds(pl.multiple_of((1 - c) * own * rank, own * rank), own * rank)

    lax.fori_loop(0, blocks // 2, pick_other, 0)

    for d in range(1, n_y):
        arrived(gram_in.at[d - 1], g_send.at[d - 1], g_recv.at[d - 1], y_peers[d - 1])
    piece = gram_part[x]
    for d in range(1, n_y):
        piece = piece + gram_in[d - 1]
    gram_all[c, x] = piece
    for k in range(len(around)):
        send(gram_all.at[c, x], gram_all.at[c, x], h_send.at[k], h_recv.at[k], around_peers[k])

    lax.fori_loop(blocks // 2, blocks - 1, pick_other, 0)
    look_up(other, blocks - 1, finish_other)
    for side in range(2):
        held = range(side * n_y // 2, (side + 1) * n_y // 2)
        add_users(blocks - 1, slice(held.start, held.stop))
        for d in far_y:
            if (d - 2) % n_y in held:
                send(total.at[(d - 2) % n_y], rows_in.at[d - 1], m_send.at[d - 1], m_recv.at[d - 1], y_peers[d - 1])

    for k, (dx, dc) in enumerate(around):
        spot = gram_all.at[core_at(dc), x_at((N_X - dx) % N_X)]
        arrived(spot, h_send.at[k], h_recv.at[k], around_peers[k])
    item_gram = gram_all[0]
    for core in range(1, N_CORE):
        item_gram = item_gram + gram_all[core]
    inverse = invert_spd(item_gram.reshape(rank, rank) * week_gram)

    for d in range(1, n_y):
        arrived(rows_in.at[d - 1], m_send.at[d - 1], m_recv.at[d - 1], y_peers[d - 1])
    rows = total[(0 - 2) % n_y]
    for d in range(1, n_y):
        rows = rows + rows_in[d - 1]
    out_ref[...] = jnp.dot(rows, inverse, preferred_element_type=F32, precision=lax.Precision.HIGHEST)

    for copy in pending:
        copy.wait_send()
    for d in range(1, N_X):
        slab = table.at[c, 0]
        pltpu.make_async_remote_copy(
            src_ref=slab, dst_ref=slab, send_sem=x_send.at[d - 1], recv_sem=x_recv.at[d - 1],
            device_id=x_peers[d - 1], device_id_type=MESH,
        ).wait_send()


def local(n_grid, n_y, user_index, item_index, week_index, counts, item_factor, week_factor):
    n_all = user_index.shape[0]
    groups = n_all // LANES
    per, rank = item_factor.shape
    n_z = n_grid // (N_X * N_CORE)
    n_item = per * n_grid
    n_lo = n_item // HI
    n_week = week_factor.shape[0] * n_y
    u_dev = 64
    users = u_dev * n_y
    dma = pltpu.SemaphoreType.DMA
    return pl.pallas_call(
        functools.partial(kernel, n_z, n_y),
        out_shape=jax.ShapeDtypeStruct((u_dev, rank), F32),
        in_specs=[pl.BlockSpec(memory_space=pltpu.MemorySpace.HBM)] * 6,
        out_specs=pl.BlockSpec(memory_space=pltpu.VMEM),
        scratch_shapes=[
            pltpu.VMEM((groups, LANES), jnp.int32),
            pltpu.VMEM((groups, LANES), jnp.int32),
            pltpu.VMEM((groups, LANES), jnp.int32),
            pltpu.VMEM((groups, LANES), BF16),
            pltpu.VMEM(item_factor.shape, BF16),
            pltpu.VMEM(week_factor.shape, BF16),
            pltpu.VMEM((groups, LANES), F32),
            pltpu.VMEM((N_CORE, N_X, n_z, per, rank), BF16),
            pltpu.VMEM((n_y,) + week_factor.shape, BF16),
            pltpu.VMEM((n_lo, n_all), BF16),
            pltpu.VMEM((users, n_all), BF16),
            pltpu.VMEM((rank, n_all), F32),
            pltpu.VMEM((rank, n_all), BF16),
            pltpu.VMEM((HI * rank, n_lo), BF16),
            pltpu.VMEM((WEEK_HI * rank, n_week // WEEK_HI), BF16),
            pltpu.VMEM((max(n_lo, users), LANES), jnp.int16),
            pltpu.VMEM((groups, LANES), jnp.int32),
            pltpu.VMEM((groups, LANES), jnp.int32),
            pltpu.VMEM((n_y, u_dev, rank), F32),
            pltpu.VMEM((N_X, rank // N_X, rank), F32),
            pltpu.VMEM((n_y - 1, rank // N_X, rank), F32),
            pltpu.VMEM((N_CORE, N_X, rank // N_X, rank), F32),
            pltpu.VMEM((n_y - 1, u_dev, rank), F32),
        ]
        + [dma((6,))]
        + [dma((n_z - 1,))] * 2
        + [dma((N_X - 1,))] * 2
        + [dma((N_X,))] * 2
        + [dma((n_y - 1,))] * 4
        + [dma((N_X * N_CORE - 1,))] * 2
        + [dma((n_y - 1,))] * 2,
        compiler_params=pltpu.CompilerParams(
            collective_id=0, has_side_effects=True, vmem_limit_bytes=62914560
        ),
        name="mttkrp_solve",
    )(
        user_index.reshape(groups, LANES),
        item_index.reshape(groups, LANES),
        week_index.reshape(groups, LANES),
        counts.reshape(groups, LANES),
        item_factor,
        week_factor,
    )


def solution(mesh):
    return jax.shard_map(
        functools.partial(local, mesh.shape["grid"], mesh.shape["slab"]),
        mesh=mesh,
        in_specs=(
            P(("grid", "slab")),
            P(("grid", "slab")),
            P(("grid", "slab")),
            P(("grid", "slab")),
            P(("grid", "slab"), None),
            P("slab", None),
        ),
        out_specs=P(("grid", "slab"), None),
        check_vma=False,
    )
```
